128 devices in a mesh: row: 16 (over y, x), col: 8 (over z, core).
Axes of the slice: x: 4, y: 4, z: 4, core: 2. Of those that a mesh axis runs over, the one named last changes fastest.
Arguments:
- a_blocks: bfloat16 [4096, 16, 128, 128], P(('row', 'col')), may hold values from -0.0625 to 0.0625
- omega: bfloat16 [32768, 256], P('col'), may hold values from -6 to 6
- route_dest: int32 [4096, 1], P(('row', 'col')), may hold values from 0 to 15; in each aligned block of 32 rows (0 to 31, 32 to 63, ...) at most 4 rows name the same one
- row_target: int32 [4096], P(('row', 'col')), may hold values from 0 to 63
- col_target: int32 [4096, 16], P(('row', 'col')), may hold values from 0 to 31
Outputs:
- basis: float32 [131072, 256], P(('row', 'col'))
- factor: float32 [256, 256], replicated
The draws below stay inside these ranges and needn't reach their ends.
Inputs may be any that keep to these rules, and one draw needn't show every extreme that they name: `route_dest`: among the 32 rows of one device no value appears more than 4 times, and in some device's rows one value appears exactly 4 times.
All inputs are finite; a program needn't handle non-finite values.
Results may differ from the reference program's by a relative error of at most 0.003.
Values may be sent and summed in bfloat16 or wider, within the bound.
No kernel may reach another device: no remote copies, remote signals or barrier semaphores. Data moves between devices by JAX's collectives and lax.ppermute only.
A program may use at most 192 MiB of HBM per device.

```python
import math
import jax
import jax.numpy as jnp
import numpy as np
from jax import lax

BS = 128
SKETCH = 256
RB_DEV = 8
NT = 32
GRP = 16
CB_DEV = 32
CAP = 4
TARGETS = 4096
OMEGA_ROWS = 32768
N_ROW = 16
N_COL = 8


def place_ends(result, own_key, least, top_value):
    extent = result.shape
    index_at = [jax.random.randint(jax.random.fold_in(own_key, axis), (), 0, extent[axis]) for axis in range(len(extent))]
    result = result.at[tuple(index_at)].set(least)
    longest = extent.index(max(extent))
    index_at[longest] = (index_at[longest] + 1) % extent[longest]
    return result.at[tuple(index_at)].set(top_value)


def block_levels(key, extent, cuts, smallest, high):
    level = 1.0
    for dim, blocks in cuts:
        heights = jax.random.uniform(jax.random.fold_in(jax.random.fold_in(key, 6), dim), (blocks,), jnp.float32, smallest / len(cuts), high / len(cuts))
        level = level * jnp.repeat(jnp.exp(heights), extent[dim] // blocks).reshape((-1,) + (1,) * (len(extent) - 1 - dim))
    return level


def assign_block(stream_key, own, number, rows, count, top, limit, skew):
    ranking = jax.random.permutation(stream_key, count)
    crowded, usual = load_shares(count, rows * top, limit, skew, True), load_shares(count, rows * top, limit, skew, False)
    places = jnp.arange(count)

    def named(sizes, rotation):
        used = int((sizes > 0).sum())
        fixed = max(1, used // 4)
        passed = fixed + (places - fixed + rotation * (used - fixed)) % max(1, count - fixed)
        return jnp.zeros((count,), jnp.int32).at[ranking[jnp.where(places < fixed, places, passed)]].set(jnp.asarray(sizes, jnp.int32))

    sizes = jnp.where(number % 4 == 0, named(crowded, number // 4), named(usual, number - number // 4 - 1))
    mixed = jax.random.permutation(jax.random.fold_in(own, 3), count)
    donor, receiver = mixed[0:count // 2 * 2:2], mixed[1:count // 2 * 2:2]
    margin = jnp.minimum(sizes[donor] - 1, limit - sizes[receiver]) // 2
    margin = jnp.where((donor == ranking[0]) | (receiver == ranking[0]) | (sizes[receiver] == 0), 0, jnp.maximum(margin, 0))
    passed = jax.random.randint(jax.random.fold_in(own, 4), (count // 2,), 0, 1 << 20) % (margin + 1)
    sizes = sizes.at[donor].add(-passed).at[receiver].add(passed)
    items = jnp.searchsorted(jnp.cumsum(sizes), jnp.arange(rows * top), side="right").astype(jnp.int32)
    grid = items.reshape(top, rows).T
    grid = grid[jax.random.permutation(jax.random.fold_in(own, 1), rows)]
    rotation = jax.random.randint(jax.random.fold_in(own, 2), (rows, 1), 0, top)
    return jnp.take_along_axis(grid, (jnp.arange(top)[None, :] + rotation) % top, axis=1)


def load_shares(number_of, total, most, slope, full):
    loads = [(1 << 20) // math.isqrt(rank ** slope) + 1 for rank in range(1, number_of + 1)]
    largest = most if full else min(most, max(-(-total // number_of), total * loads[0] // sum(loads)))
    least = 1 if total - largest >= number_of - 1 else 0
    given, surplus = [largest] + [least] * (number_of - 1), total - largest - least * (number_of - 1)
    while surplus > 0:
        movable = [i for i in range(1, number_of) if given[i] < largest] or [i for i in range(1, number_of) if given[i] < most]
        mass, remaining = sum([loads[i] for i in movable]), surplus
        for i in movable:
            extra = min(most - given[i], max(1, remaining * loads[i] // mass), surplus)
            given[i] = given[i] + extra
            surplus = surplus - extra
    return np.array(given)


def bell_draw(own_key, extent, width, limit, pieces=(), held_as=jnp.bfloat16):
    gain = block_levels(own_key, extent, pieces, -0.22, 0.18) if pieces else 1.0
    result = jax.random.normal(own_key, extent, jnp.float32) * width * gain
    return jnp.minimum(jnp.maximum(result, -limit), limit).astype(held_as)


def setup_inputs(seed: int = 0) -> dict:
    seeds = jax.random.split(jax.random.key(seed), 6)
    a_blocks = bell_draw(seeds[0], (TARGETS, GRP, BS, BS), (BS * GRP * NT // RB_DEV) ** -0.5, 0.0625, ((0, 128),))
    omega = bell_draw(seeds[1], (OMEGA_ROWS, SKETCH), 1.0, 6.0, ((0, 8),))
    route_dest_keys = jax.random.split(jax.random.fold_in(seeds[2], 1), TARGETS // NT)
    route_dest_turns = jax.random.permutation(jax.random.fold_in(seeds[2], 3), TARGETS // NT)
    route_dest = jax.vmap(lambda own, number: assign_block(jax.random.fold_in(seeds[2], 2), own, number, NT, N_ROW, 1, CAP, 1))(route_dest_keys, route_dest_turns).reshape((TARGETS, 1))
    row_target = place_ends(jax.random.randint(seeds[3], (TARGETS,), 0, RB_DEV * N_COL), jax.random.fold_in(seeds[3], 1), 0, (RB_DEV * N_COL) - 1).astype(jnp.int32)
    col_target = place_ends(jax.random.randint(seeds[4], (TARGETS, GRP), 0, CB_DEV), jax.random.fold_in(seeds[4], 1), 0, CB_DEV - 1).astype(jnp.int32)
    return dict(a_blocks=a_blocks, omega=omega, route_dest=route_dest, row_target=row_target, col_target=col_target)


def reference(a_blocks, omega, route_dest, row_target, col_target):
    devices = N_ROW * N_COL
    group_blocks = RB_DEV * N_COL
    slabs = omega.reshape(N_COL, CB_DEV, BS, SKETCH)
    blocks = a_blocks.reshape(devices, NT, GRP, BS, BS)
    targets = (route_dest[:, 0] * group_blocks + row_target).astype(jnp.int32).reshape(devices, NT)
    columns = col_target.astype(jnp.int32).reshape(devices, NT, GRP)

    def add_device(carry, inputs):
        dev_blocks, dev_targets, dev_columns, device = inputs
        slab = lax.dynamic_index_in_dim(slabs, device % N_COL, 0, keepdims=False)
        picked = slab[dev_columns].astype(jnp.float32)
        partial_value = jnp.einsum('tgij,tgjk->tik', dev_blocks.astype(jnp.float32), picked, precision=lax.Precision.HIGHEST)
        rounded = lax.optimization_barrier(partial_value.astype(jnp.bfloat16))
        return (carry.at[dev_targets].add(rounded.astype(jnp.float32)), None)
    start = jnp.zeros((RB_DEV * devices, BS, SKETCH), jnp.float32)
    device_ids = jnp.arange(devices, dtype=jnp.int32)
    summed, _ = lax.scan(add_device, start, (blocks, targets, columns, device_ids))
    sketch = summed.reshape(RB_DEV * devices * BS, SKETCH)
    q_factor, r_factor = jnp.linalg.qr(sketch)
    signs = jnp.sign(jnp.diagonal(r_factor))
    q_factor = q_factor * signs[None, :]
    r_factor = r_factor * signs[:, None]
    total = float(RB_DEV * devices * BS)
    basis = (q_factor * jnp.sqrt(total)).astype(jnp.float32)
    factor = (r_factor / jnp.sqrt(total)).astype(jnp.float32)
    return (basis, factor)
```

```python
import functools

import jax
import jax.numpy as jnp
from jax import lax
from jax.experimental import pallas as pl
from jax.experimental.pallas import tpu as pltpu
from jax.sharding import PartitionSpec as P

RB_DEV = 8
CAP = 4
BS = 128
META = 16
PANEL = 32
F32 = jnp.float32
BF16 = jnp.bfloat16
HIGHEST = lax.Precision.HIGHEST
VMEM_LIMIT = 48 * 1024 * 1024


def partial_kernel(col_ref, dest_ref, row_ref, a_ref, omega_ref, out_ref, stage, meta, count, sems, meta_sem):
    step = pl.program_id(0)
    steps = pl.num_programs(0)
    group = a_ref.shape[1]
    width = omega_ref.shape[-1]

    @pl.when(step == 0)
    def _():
        meta[...] = jnp.full(meta.shape, -1.0, meta.dtype)
        for d in range(count.shape[0]):
            count[d] = 0

    dest = dest_ref[step]
    rank = count[dest]
    count[dest] = rank + 1
    here = jnp.logical_and(
        lax.broadcasted_iota(jnp.int32, (META, width), 0) == 0,
        lax.broadcasted_iota(jnp.int32, (META, width), 1) == rank,
    )
    value = jnp.full((META, width), row_ref[step], jnp.int32).astype(F32)
    meta[dest] = jnp.where(here, value, meta[dest].astype(F32)).astype(BF16)

    total = jnp.zeros((BS, width), F32)
    for g in range(0, group, 2):
        left = jnp.concatenate([a_ref[0, g], a_ref[0, g + 1]], axis=1)
        right = jnp.concatenate(
            [omega_ref[col_ref[step, g]], omega_ref[col_ref[step, g + 1]]], axis=0
        )
        total = total + jnp.dot(left, right, preferred_element_type=F32)

    slot = lax.rem(step, 2)

    def copy_out(which, d, r):
        return pltpu.make_async_copy(
            stage.at[which],
            out_ref.at[d, pl.ds(pl.multiple_of(r * BS, BS), BS), :],
            sems.at[which],
        )

    @pl.when(step >= 2)
    def _():
        copy_out(slot, 0, 0).wait()

    stage[slot] = total.astype(BF16)
    copy_out(slot, dest, rank).start()

    @pl.when(step == steps - 1)
    def _():
        last = pltpu.make_async_copy(meta, out_ref.at[:, pl.ds(CAP * BS, META), :], meta_sem)
        last.start()
        copy_out(1 - slot, 0, 0).wait()
        copy_out(slot, 0, 0).wait()
        last.wait()


def partials(a_blocks, omega, route_dest, row_target, col_target, owners):
    targets, group = col_target.shape
    width = omega.shape[1]
    slab = omega.reshape(-1, BS, width)
    return pl.pallas_call(
        partial_kernel,
        grid_spec=pltpu.PrefetchScalarGridSpec(
            num_scalar_prefetch=3,
            grid=(targets,),
            in_specs=[
                pl.BlockSpec((1, group, BS, BS), lambda t, *_: (t, 0, 0, 0)),
                pl.BlockSpec(slab.shape, lambda t, *_: (0, 0, 0)),
            ],
            out_specs=pl.BlockSpec(memory_space=pl.ANY),
            scratch_shapes=[
                pltpu.VMEM((2, BS, width), BF16),
                pltpu.VMEM((owners, META, width), BF16),
                pltpu.SMEM((owners,), jnp.int32),
                pltpu.SemaphoreType.DMA((2,)),
                pltpu.SemaphoreType.DMA,
            ],
        ),
        out_shape=jax.ShapeDtypeStruct((owners, CAP * BS + META, width), BF16),
        compiler_params=pltpu.CompilerParams(vmem_limit_bytes=VMEM_LIMIT),
        name="partials",
    )(col_target, route_dest[:, 0], row_target, a_blocks, slab)


def slot_sum_kernel(rows_ref, place_ref, got_ref, send_ref, keep_ref, acc):
    step = pl.program_id(0)
    blocks = acc.shape[0]

    @pl.when(step == 0)
    def _():
        def clear(b, carry):
            acc[b] = jnp.zeros(acc.shape[1:], F32)
            return carry

        lax.fori_loop(0, blocks, clear, 0)

    for r in range(CAP):
        row = rows_ref[step * CAP + r]

        @pl.when(row >= 0)
        def _():
            acc[row] = acc[row] + got_ref[0, r * BS : (r + 1) * BS, :].astype(F32)

    @pl.when(step == pl.num_programs(0) - 1)
    def _():
        z, core = place_ref[0], place_ref[1]

        def write(k, carry):
            d = k // RB_DEV
            chip = lax.rem(z + d, 4)
            base = chip * (2 * RB_DEV) + lax.rem(k, RB_DEV)
            send_ref[k] = acc[base + (1 - core) * RB_DEV].astype(BF16)
            keep_ref[k] = acc[base + core * RB_DEV]
            return carry

        lax.fori_loop(0, 4 * RB_DEV, write, 0)


def slot_sums(rows, place, got):
    owners, _, width = got.shape
    half = 4 * RB_DEV
    return pl.pallas_call(
        slot_sum_kernel,
        grid_spec=pltpu.PrefetchScalarGridSpec(
            num_scalar_prefetch=2,
            grid=(owners,),
            in_specs=[pl.BlockSpec((1, CAP * BS + META, width), lambda s, *_: (s, 0, 0))],
            out_specs=[
                pl.BlockSpec((half, BS, width), lambda s, *_: (0, 0, 0)),
                pl.BlockSpec((half, BS, width), lambda s, *_: (0, 0, 0)),
            ],
            scratch_shapes=[pltpu.VMEM((2 * half, BS, width), F32)],
        ),
        out_shape=[
            jax.ShapeDtypeStruct((half, BS, width), BF16),
            jax.ShapeDtypeStruct((half, BS, width), F32),
        ],
        compiler_params=pltpu.CompilerParams(vmem_limit_bytes=VMEM_LIMIT),
        name="slot_sums",
    )(rows, place, got)


def gram_kernel(place_ref, own_ref, core_ref, z1_ref, z2_ref, z3_ref, sketch_ref, send_ref, keep_ref, gram):
    z, core = place_ref[0], place_ref[1]
    sketch_ref[...] = (
        (own_ref[...] + core_ref[...].astype(F32))
        + (z1_ref[...].astype(F32) + z2_ref[...].astype(F32))
        + z3_ref[...].astype(F32)
    )
    sketch = sketch_ref[...]
    gram[...] = lax.dot_general(
        sketch, sketch, (((0,), (0,)), ((), ())), precision=HIGHEST, preferred_element_type=F32
    )
    part = send_ref.shape[0] // 4
    half = send_ref.shape[0]
    for d in range(4):
        chip = lax.rem(z + d, 4)
        send_ref[d * part : (d + 1) * part, :] = gram[
            pl.ds(pl.multiple_of((1 - core) * half + chip * part, part), part), :
        ]
        keep_ref[d * part : (d + 1) * part, :] = gram[
            pl.ds(pl.multiple_of(core * half + chip * part, part), part), :
        ]


def gram_halves(place, own, core_part, others):
    rows, width = own.shape
    whole = pl.BlockSpec(memory_space=pltpu.VMEM)
    return pl.pallas_call(
        gram_kernel,
        in_specs=[pl.BlockSpec(memory_space=pltpu.SMEM)] + [whole] * 5,
        out_specs=[whole] * 3,
        out_shape=[
            jax.ShapeDtypeStruct((rows, width), F32),
            jax.ShapeDtypeStruct((width // 2, width), F32),
            jax.ShapeDtypeStruct((width // 2, width), F32),
        ],
        scratch_shapes=[pltpu.VMEM((width, width), F32)],
        compiler_params=pltpu.CompilerParams(vmem_limit_bytes=VMEM_LIMIT),
        name="sum_gram",
    )(place, own, core_part, *others)


def factor_kernel(scale, place_ref, *refs):
    pieces, (sketch_ref, basis_ref, factor_ref, work) = refs[:8], refs[8:]
    z, core = place_ref[0], place_ref[1]
    part, n = pieces[0].shape
    for c in range(2):
        side = core if c == 0 else 1 - core
        for d in range(4):
            chip = lax.rem(z - d + 4, 4)
            work[pl.ds(pl.multiple_of((side * 4 + chip) * part, part), part), 0:n] = pieces[c * 4 + d][...]
    work[:, n : 2 * n] = (
        lax.broadcasted_iota(jnp.int32, (n, n), 0) == lax.broadcasted_iota(jnp.int32, (n, n), 1)
    ).astype(F32)
    below = lax.broadcasted_iota(jnp.int32, (PANEL, 1), 0)
    for j in range(0, n, PANEL):
        first, last = (j // BS) * BS, n + (j // BS) * BS + BS
        panel = [work[j : j + PANEL, t : t + BS] for t in range(first, last, BS)]
        lane = j - first
        for k in range(PANEL):
            column = panel[0][:, lane + k : lane + k + 1]
            inv_root = lax.rsqrt(column[k : k + 1, :])
            ratio = jnp.where(below > k, column * inv_root, 0.0)
            for i in range(len(panel)):
                row = panel[i][k : k + 1, :] * inv_root
                panel[i] = jnp.where(below == k, row, panel[i] - ratio * row)
        for i, t in enumerate(range(first, last, BS)):
            work[j : j + PANEL, t : t + BS] = panel[i]
        if j + PANEL < n:
            done = work[j : j + PANEL, first:last]
            work[j + PANEL : n, first:last] -= lax.dot_general(
                work[j : j + PANEL, j + PANEL : n],
                done,
                (((0,), (0,)), ((), ())),
                precision=HIGHEST,
                preferred_element_type=F32,
            )
    upper = lax.broadcasted_iota(jnp.int32, (n, n), 0) <= lax.broadcasted_iota(jnp.int32, (n, n), 1)
    factor_ref[...] = jnp.where(upper, work[:, 0:n], 0.0) * (1.0 / scale)
    inverse = work[:, n : 2 * n] * scale
    basis_ref[...] = lax.dot_general(
        sketch_ref[...], inverse, (((1,), (1,)), ((), ())), precision=HIGHEST, preferred_element_type=F32
    )


def factors(scale, place, pieces, sketch):
    rows, width = sketch.shape
    whole = pl.BlockSpec(memory_space=pltpu.VMEM)
    return pl.pallas_call(
        functools.partial(factor_kernel, scale),
        in_specs=[pl.BlockSpec(memory_space=pltpu.SMEM)] + [whole] * 9,
        out_specs=[whole] * 2,
        out_shape=[
            jax.ShapeDtypeStruct((rows, width), F32),
            jax.ShapeDtypeStruct((width, width), F32),
        ],
        scratch_shapes=[pltpu.VMEM((width, 2 * width), F32)],
        compiler_params=pltpu.CompilerParams(vmem_limit_bytes=VMEM_LIMIT),
        name="factor_basis",
    )(place, *pieces, sketch)


def other_core(value):
    return lax.ppermute(value, "col", [(i, i ^ 1) for i in range(8)])


def along_z(value, d):
    return lax.ppermute(value, "col", [(i, (i + 2 * d) % 8) for i in range(8)])


def along_y(value, d):
    return lax.ppermute(value, "row", [(i, (i + 4 * d) % 16) for i in range(16)])


def along_x(value, d):
    return lax.ppermute(value, "row", [(i, i // 4 * 4 + (i + d) % 4) for i in range(16)])


def summed(value, along):
    one, two, three = (along(value, d) for d in (1, 2, 3))
    return (value + two) + (one + three)


def body(scale, a_blocks, omega, route_dest, row_target, col_target):
    width = omega.shape[1]
    owners = lax.axis_size("row")
    col = lax.axis_index("col")
    place = jnp.stack([col // 2, col % 2]).astype(jnp.int32)
    send = partials(a_blocks, omega, route_dest, row_target, col_target, owners)
    got = lax.all_to_all(send, "row", split_axis=0, concat_axis=0, tiled=True)
    rows = got[:, CAP * BS, :CAP].reshape(-1).astype(jnp.int32)
    to_core, own = slot_sums(rows, place, got)
    from_core = other_core(to_core)
    per_chip = RB_DEV
    half = 4 * RB_DEV
    others = [
        along_z(
            (
                own[d * per_chip : (d + 1) * per_chip]
                + from_core[d * per_chip : (d + 1) * per_chip].astype(F32)
            ).astype(BF16),
            d,
        ).reshape(-1, width)
        for d in (1, 2, 3)
    ]
    sketch, gram_send, gram_keep = gram_halves(
        place,
        own[:per_chip].reshape(-1, width),
        from_core[:per_chip].reshape(-1, width),
        others,
    )
    gram = gram_keep + other_core(gram_send)
    part = gram.shape[0] // 4
    piece = gram[:part]
    moved = [along_z(gram[d * part : (d + 1) * part], d) for d in (1, 2, 3)]
    piece = (piece + moved[1]) + (moved[0] + moved[2])
    piece = summed(summed(piece, along_y), along_x)
    mine = [piece] + [along_z(piece, d) for d in (1, 2, 3)]
    pieces = mine + [other_core(p) for p in mine]
    return tuple(factors(scale, place, pieces, sketch))


def solution(mesh):
    rows_total = mesh.shape["row"] * mesh.shape["col"] * RB_DEV * BS
    return jax.shard_map(
        functools.partial(body, float(rows_total) ** 0.5),
        mesh=mesh,
        in_specs=(
            P(("row", "col"), None, None, None),
            P("col", None),
            P(("row", "col"), None),
            P(("row", "col")),
            P(("row", "col"), None),
        ),
        out_specs=(P(("row", "col"), None), P()),
        check_vma=False,
    )
```

```python
import functools

import jax
import jax.numpy as jnp
from jax import lax
from jax.experimental import pallas as pl
from jax.experimental.pallas import tpu as pltpu
from jax.sharding import PartitionSpec as P

RB_DEV = 8
CAP = 4
BS = 128
META = 16
SLOT_ROWS = CAP * BS + META
CHUNKS = 2
PANEL = 32
UNROLL = 4
AHEAD = 3
SIDE = 4
OWNERS = SIDE * SIDE
HALF = SIDE * RB_DEV
F32 = jnp.float32
BF16 = jnp.bfloat16
HIGHEST = lax.Precision.HIGHEST
MIB = 1024 * 1024
WHOLE = pl.BlockSpec(memory_space=pltpu.VMEM)
SCALARS = pl.BlockSpec(memory_space=pltpu.SMEM)
IN_HBM = pl.BlockSpec(memory_space=pltpu.HBM)


def one_of(index, low, high, act):
    if high - low == 1:
        act(low)
        return
    middle = (low + high) // 2
    lax.cond(
        index < middle,
        lambda: one_of(index, low, middle, act),
        lambda: one_of(index, middle, high, act),
    )


def partial_kernel(index_ref, place_ref, a_ref, omega_ref, *refs):
    outs, scratch = refs[: CHUNKS * SIDE], refs[CHUNKS * SIDE :]
    blocks, slab, stage, meta, rows, count, a_sems, slab_sem, out_sems, meta_sems = scratch
    targets, group = blocks.shape[:2]
    width = slab.shape[-1] // CHUNKS
    core, y, x = place_ref[1], place_ref[2], place_ref[3]
    slab_copy = pltpu.make_async_copy(omega_ref, slab, slab_sem)
    slab_copy.start()

    def load(step):
        some = pl.ds(step * UNROLL, UNROLL)
        return pltpu.make_async_copy(a_ref.at[some], blocks.at[some], a_sems.at[step])

    for step in range(AHEAD):
        load(step).start()

    def clear(o, carry):
        count[o] = 0
        for r in range(CAP):
            rows[o, r] = -1
        return carry

    lax.fori_loop(0, OWNERS, clear, 0)
    slab_copy.wait()

    def copy_out(t, first, second, rank, c):
        return pltpu.make_async_copy(
            stage.at[t, :, pl.ds(c * width, width)],
            outs[c * SIDE + first].at[second, pl.ds(pl.multiple_of(rank * BS, BS), BS), :],
            out_sems.at[c, t],
        )

    def several(step, carry):
        @pl.when(step + AHEAD < targets // UNROLL)
        def _():
            load(step + AHEAD).start()

        load(step).wait()
        for i in range(UNROLL):
            t = step * UNROLL + i
            left = jnp.concatenate([blocks[t, g] for g in range(group)], axis=1)
            right = jnp.concatenate([slab[index_ref[g, t]] for g in range(group)], axis=0)
            stage[t] = jnp.dot(left, right, preferred_element_type=F32).astype(BF16)
        for i in range(UNROLL):
            t = step * UNROLL + i
            dest = index_ref[group, t]
            dy, dx = (dest // SIDE - y) & (SIDE - 1), (dest - x) & (SIDE - 1)
            first, second = jnp.where(core == 0, dy, dx), jnp.where(core == 0, dx, dy)
            owner = first * SIDE + second
            rank = count[owner]
            count[owner] = rank + 1
            rows[owner, rank] = index_ref[group + 1, t]

            def send(d, t=t, second=second, rank=rank):
                for c in range(CHUNKS):
                    copy_out(t, d, second, rank, c).start()

            one_of(first, 0, SIDE, send)
        return carry

    lax.fori_loop(0, targets // UNROLL, several, 0)
    lane = lax.broadcasted_iota(jnp.int32, (META, width), 1)
    for o in range(OWNERS):
        values = jnp.full((META, width), -1, jnp.int32)
        for r in range(CAP):
            values = jnp.where(lane == r, rows[o, r], values)
        meta[o] = values.astype(F32).astype(BF16)
    tails = [
        pltpu.make_async_copy(
            meta.at[pl.ds(d * SIDE, SIDE)],
            outs[c * SIDE + d].at[:, pl.ds(CAP * BS, META), :],
            meta_sems.at[c, d],
        )
        for c in range(CHUNKS)
        for d in range(SIDE)
    ]
    for tail in tails:
        tail.start()

    def finish(t, carry):
        for c in range(CHUNKS):
            copy_out(t, 0, 0, 0, c).wait()
        return carry

    lax.fori_loop(0, targets, finish, 0)
    for tail in tails:
        tail.wait()


def partials(a_blocks, omega, route_dest, row_target, col_target, place):
    targets = col_target.shape[0]
    width = omega.shape[1]
    slab = omega.reshape(-1, BS, width)
    indices = jnp.concatenate([col_target.T, route_dest.T, row_target[None, :]])
    out = jax.ShapeDtypeStruct((SIDE, SLOT_ROWS, width // CHUNKS), BF16)
    outs = pl.pallas_call(
        partial_kernel,
        in_specs=[SCALARS] * 2 + [IN_HBM] * 2,
        out_specs=[pl.BlockSpec(memory_space=pl.ANY)] * (CHUNKS * SIDE),
        out_shape=[out] * (CHUNKS * SIDE),
        scratch_shapes=[
            pltpu.VMEM(a_blocks.shape, BF16),
            pltpu.VMEM(slab.shape, BF16),
            pltpu.VMEM((targets, BS, width), BF16),
            pltpu.VMEM((OWNERS, META, width // CHUNKS), BF16),
            pltpu.SMEM((OWNERS, CAP), jnp.int32),
            pltpu.SMEM((OWNERS,), jnp.int32),
            pltpu.SemaphoreType.DMA((targets // UNROLL,)),
            pltpu.SemaphoreType.DMA,
            pltpu.SemaphoreType.DMA((CHUNKS, targets)),
            pltpu.SemaphoreType.DMA((CHUNKS, SIDE)),
        ],
        compiler_params=pltpu.CompilerParams(vmem_limit_bytes=48 * MIB),
        name="partials",
    )(indices, place, a_blocks, slab)
    return [outs[c * SIDE : (c + 1) * SIDE] for c in range(CHUNKS)]


def slot_sum_kernel(place_ref, *refs):
    got, (send_ref, acc, ints, rows, sem) = refs[: 2 * SIDE - 1], refs[2 * SIDE - 1 :]
    z, core = place_ref[0], place_ref[1]
    pieces = [(ref, 0) for ref in got[:SIDE]] + [(ref, i) for ref in got[SIDE:] for i in range(SIDE)]
    for s, (ref, i) in enumerate(pieces):
        tile = ref[i, CAP * BS : SLOT_ROWS, 0:BS].astype(F32)
        row = tile[0:1, :].astype(jnp.int32)
        side = (row // RB_DEV) & 1
        chip = (row // (2 * RB_DEV) - z) & (SIDE - 1)
        place = jnp.where(side == core, 0, HALF) + chip * RB_DEV + (row & (RB_DEV - 1))
        ints[s : s + 1, :] = jnp.where(row < 0, row, place)
    copy = pltpu.make_async_copy(ints, rows, sem)
    copy.start()

    def clear(b, carry):
        acc[b] = jnp.zeros(acc.shape[1:], F32)
        return carry

    lax.fori_loop(0, 2 * HALF, clear, 0, unroll=2)
    copy.wait()
    for s, (ref, i) in enumerate(pieces):
        for r in range(CAP):
            place = rows[s, r]

            @pl.when(place >= 0)
            def _():
                acc[place] = acc[place] + ref[i, r * BS : (r + 1) * BS, :].astype(F32)

    def write(k, carry):
        send_ref[k] = acc[HALF + k].astype(BF16)
        return carry

    lax.fori_loop(0, HALF, write, 0, unroll=2)


def slot_sums(place, got):
    width = got[0].shape[2]
    return pl.pallas_call(
        slot_sum_kernel,
        in_specs=[SCALARS] + [WHOLE] * len(got),
        out_specs=[WHOLE] * 2,
        out_shape=[
            jax.ShapeDtypeStruct((HALF, BS, width), BF16),
            jax.ShapeDtypeStruct((2 * HALF, BS, width), F32),
        ],
        scratch_shapes=[
            pltpu.VMEM((OWNERS, BS), jnp.int32),
            pltpu.SMEM((OWNERS, BS), jnp.int32),
            pltpu.SemaphoreType.DMA,
        ],
        compiler_params=pltpu.CompilerParams(vmem_limit_bytes=22 * MIB),
        name="slot_sums",
    )(place, *got)


def gram_kernel(place_ref, *refs):
    parts, (sketch_ref, send_ref, keep_ref, gram) = refs[: 5 * CHUNKS], refs[5 * CHUNKS :]
    core = place_ref[1]
    width = parts[0].shape[1]
    for c in range(CHUNKS):
        own, from_core, one, two, three = (ref[...].astype(F32) for ref in parts[5 * c : 5 * c + 5])
        sketch_ref[:, c * width : (c + 1) * width] = (own + from_core) + (one + three) + two
    sketch = sketch_ref[...]
    gram[...] = lax.dot_general(
        sketch, sketch, (((0,), (0,)), ((), ())), precision=HIGHEST, preferred_element_type=F32
    )
    half = send_ref.shape[0]
    send_ref[...] = gram[pl.ds(pl.multiple_of((1 - core) * half, half), half), :]
    keep_ref[...] = gram[pl.ds(pl.multiple_of(core * half, half), half), :]


def gram_halves(place, parts):
    rows = RB_DEV * BS
    width = CHUNKS * parts[0].shape[1]
    return pl.pallas_call(
        gram_kernel,
        in_specs=[SCALARS] + [WHOLE] * (5 * CHUNKS),
        out_specs=[WHOLE] * 3,
        out_shape=[
            jax.ShapeDtypeStruct((rows, width), F32),
            jax.ShapeDtypeStruct((width // 2, width), F32),
            jax.ShapeDtypeStruct((width // 2, width), F32),
        ],
        scratch_shapes=[pltpu.VMEM((width, width), F32)],
        compiler_params=pltpu.CompilerParams(vmem_limit_bytes=20 * MIB),
        name="sum_gram",
    )(place, *parts)


def small_factor(block):
    n = len(block)
    low = [list(row) for row in block]
    inv = [None] * n
    for k in range(n):
        inv[k] = lax.rsqrt(low[k][k])
        for i in range(k + 1, n):
            low[i][k] = low[i][k] * inv[k]
        for j in range(k + 1, n):
            for i in range(j, n):
                low[i][j] = low[i][j] - low[i][k] * low[j][k]
    out = [[None] * n for _ in range(n)]
    for j in range(n):
        out[j][j] = inv[j]
        for i in range(j + 1, n):
            s = low[i][j] * out[j][j]
            for m in range(j + 1, i):
                s = s + low[i][m] * out[m][j]
            out[i][j] = -(s * inv[i])
    return out


def wide(value):
    return jnp.broadcast_to(value, (8, BS))


def factor_panel(panel, lane):
    sub = lax.broadcasted_iota(jnp.int32, (8, BS), 0)
    for g in range(len(panel)):
        at = lane + 8 * g
        cols = [wide(panel[g][0][:, at + c : at + c + 1]) for c in range(8)]
        inverse = small_factor([[wide(cols[c][r : r + 1, :]) for c in range(r + 1)] for r in range(8)])
        spread = []
        for k in range(8):
            value = inverse[7][k]
            for r in range(6, k - 1, -1):
                value = jnp.where(sub == r, inverse[r][k], value)
            spread.append(jnp.where(sub >= k, value, 0.0))
        done = []
        for tile in panel[g]:
            total = spread[0] * wide(tile[0:1, :])
            for k in range(1, 8):
                total = total + spread[k] * wide(tile[k : k + 1, :])
            done.append(total)
        panel[g] = done
        done_rows = [[wide(tile[k : k + 1, :]) for k in range(8)] for tile in done]
        for h in range(g + 1, len(panel)):
            cols = [wide(panel[h][0][:, at + c : at + c + 1]) for c in range(8)]
            for k in range(8):
                ratio = cols[0] * inverse[k][0]
                for m in range(1, k + 1):
                    ratio = ratio + cols[m] * inverse[k][m]
                for t in range(len(done)):
                    panel[h][t] = panel[h][t] - ratio * done_rows[t][k]


def factor_kernel(scale, place_ref, mine_ref, other_ref, sketch_ref, basis_ref, factor_ref, work):
    core = place_ref[1]
    n = mine_ref.shape[1]
    half = n // 2
    work[pl.ds(pl.multiple_of(core * half, half), half), 0:n] = mine_ref[...]
    work[pl.ds(pl.multiple_of((1 - core) * half, half), half), 0:n] = other_ref[...]
    down = lax.broadcasted_iota(jnp.int32, (n, n), 0)
    across = lax.broadcasted_iota(jnp.int32, (n, n), 1)
    work[:, n : 2 * n] = (down == across).astype(F32)
    for j in range(0, n, PANEL):
        first, last = (j // BS) * BS, n + (j // BS) * BS + BS
        tiles = range(first, last, BS)
        panel = [[work[i : i + 8, t : t + BS] for t in tiles] for i in range(j, j + PANEL, 8)]
        factor_panel(panel, j - first)
        for g, group in enumerate(panel):
            for t, tile in zip(tiles, group):
                work[j + 8 * g : j + 8 * g + 8, t : t + BS] = tile
        if j + PANEL < n:
            work[j + PANEL : n, first:last] -= lax.dot_general(
                work[j : j + PANEL, j + PANEL : n],
                work[j : j + PANEL, first:last],
                (((0,), (0,)), ((), ())),
                precision=HIGHEST,
                preferred_element_type=F32,
            )
    factor_ref[...] = jnp.where(down <= across, work[:, 0:n], 0.0) * (1.0 / scale)
    inverse = work[:, n : 2 * n] * scale
    basis_ref[...] = lax.dot_general(
        sketch_ref[...], inverse, (((1,), (1,)), ((), ())), precision=HIGHEST, preferred_element_type=F32
    )


def factors(scale, place, mine, other, sketch):
    rows, width = sketch.shape
    return pl.pallas_call(
        functools.partial(factor_kernel, scale),
        in_specs=[SCALARS] + [WHOLE] * 3,
        out_specs=[WHOLE] * 2,
        out_shape=[
            jax.ShapeDtypeStruct((rows, width), F32),
            jax.ShapeDtypeStruct((width, width), F32),
        ],
        scratch_shapes=[pltpu.VMEM((width, 2 * width), F32)],
        compiler_params=pltpu.CompilerParams(vmem_limit_bytes=16 * MIB),
        name="factor_basis",
    )(place, mine, other, sketch)


def other_core(value):
    return lax.ppermute(value, "col", [(i, i ^ 1) for i in range(2 * SIDE)])


def moved(value, target):
    pairs = []
    for y in range(SIDE):
        for x in range(SIDE):
            for z in range(SIDE):
                for core in range(2):
                    to_y, to_x, to_z = target(core, (y, x, z))
                    source = ((y * SIDE + x) * SIDE + z) * 2 + core
                    pairs.append((source, ((to_y * SIDE + to_x) * SIDE + to_z) * 2 + core))
    return lax.ppermute(value, ("row", "col"), pairs)


def along(value, axes, step):
    def target(core, chip):
        return tuple(step(at) if axis == axes[core] else at for axis, at in enumerate(chip))

    return moved(value, target)


def ahead(value, axes, d):
    return along(value, axes, lambda at: (at + d) % SIDE)


def summed(value):
    for axes in ((2, 0), (0, 1), (1, 2)):
        one, three, two = (ahead(value, axes, d) for d in (1, 3, 2))
        value = (value + two) + (one + three)
    return value


def body(scale, a_blocks, omega, route_dest, row_target, col_target):
    row, col = lax.axis_index("row"), lax.axis_index("col")
    place = jnp.stack([col // 2, col % 2, row // SIDE, row % SIDE]).astype(jnp.int32)
    sends = partials(a_blocks, omega, route_dest, row_target, col_target, place)
    parts = []
    for c, send in enumerate(sends):
        near = [send[0]] + [ahead(send[d], (0, 1), d) for d in (1, 3, 2)]
        across = [jnp.stack([part[d] for part in near]) for d in (1, 3, 2)]
        far = [ahead(value, (1, 0), d) for d, value in zip((1, 3, 2), across)]
        kept, leaving = core_sums(place, near + far)
        parts = parts + kept + sent_along_z(leaving)
    sketch, gram_send, gram_keep = gram_halves(place, parts)
    gram = summed(gram_keep + other_core(gram_send))
    return tuple(factors(scale, place, gram, other_core(gram), sketch))


def core_sums(place, got):
    to_core, own = slot_sums(place, got)
    width = own.shape[-1]
    own, from_core = own.reshape(2 * SIDE, -1, width), other_core(to_core).reshape(SIDE, -1, width)
    leaving = [(own[d] + from_core[d].astype(F32)).astype(BF16) for d in (1, 3, 2)]
    return [own[0], from_core[0]], leaving


def sent_along_z(leaving):
    return [ahead(value, (2, 2), d) for d, value in zip((1, 3, 2), leaving)]


def solution(mesh):
    rows_total = mesh.shape["row"] * mesh.shape["col"] * RB_DEV * BS
    return jax.shard_map(
        functools.partial(body, float(rows_total) ** 0.5),
        mesh=mesh,
        in_specs=(
            P(("row", "col"), None, None, None),
            P("col", None),
            P(("row", "col"), None),
            P(("row", "col")),
            P(("row", "col"), None),
        ),
        out_specs=(P(("row", "col"), None), P()),
        check_vma=False,
    )
```

```python
import functools

import jax
import jax.numpy as jnp
from jax import lax
from jax.experimental import pallas as pl
from jax.experimental.pallas import tpu as pltpu
from jax.sharding import PartitionSpec as P

RB_DEV = 8
CAP = 4
BS = 128
META = 16
SLOT_ROWS = CAP * BS + META
CHUNKS = 2
PANEL = 32
UNROLL = 4
AHEAD = 3
SIDE = 4
OWNERS = SIDE * SIDE
HALF = SIDE * RB_DEV
F32 = jnp.float32
BF16 = jnp.bfloat16
HIGHEST = lax.Precision.HIGHEST
MIB = 1024 * 1024
WHOLE = pl.BlockSpec(memory_space=pltpu.VMEM)
SCALARS = pl.BlockSpec(memory_space=pltpu.SMEM)
IN_HBM = pl.BlockSpec(memory_space=pltpu.HBM)


def one_of(index, low, high, act):
    if high - low == 1:
        act(low)
        return
    middle = (low + high) // 2
    lax.cond(
        index < middle,
        lambda: one_of(index, low, middle, act),
        lambda: one_of(index, middle, high, act),
    )


def partial_kernel(index_ref, place_ref, a_ref, omega_ref, *refs):
    outs, scratch = refs[: CHUNKS * SIDE], refs[CHUNKS * SIDE :]
    blocks, slab, stage, meta, rows, count, a_sems, slab_sem, out_sems, meta_sems = scratch
    targets, group = blocks.shape[:2]
    width = slab.shape[-1] // CHUNKS
    core, y, x = place_ref[1], place_ref[2], place_ref[3]
    slab_copy = pltpu.make_async_copy(omega_ref, slab, slab_sem)
    slab_copy.start()

    def load(step):
        some = pl.ds(step * UNROLL, UNROLL)
        return pltpu.make_async_copy(a_ref.at[some], blocks.at[some], a_sems.at[step])

    for step in range(AHEAD):
        load(step).start()

    def clear(o, carry):
        count[o] = 0
        for r in range(CAP):
            rows[o, r] = -1
        return carry

    lax.fori_loop(0, OWNERS, clear, 0)
    slab_copy.wait()

    def copy_out(t, first, second, rank, c):
        return pltpu.make_async_copy(
            stage.at[t, :, pl.ds(c * width, width)],
            outs[c * SIDE + first].at[second, pl.ds(pl.multiple_of(rank * BS, BS), BS), :],
            out_sems.at[c, t],
        )

    def several(step, carry):
        @pl.when(step + AHEAD < targets // UNROLL)
        def _():
            load(step + AHEAD).start()

        load(step).wait()
        for i in range(UNROLL):
            t = step * UNROLL + i
            left = jnp.concatenate([blocks[t, g] for g in range(group)], axis=1)
            right = jnp.concatenate([slab[index_ref[g, t]] for g in range(group)], axis=0)
            stage[t] = jnp.dot(left, right, preferred_element_type=F32).astype(BF16)
        for i in range(UNROLL):
            t = step * UNROLL + i
            dest = index_ref[group, t]
            dy, dx = (dest // SIDE - y) & (SIDE - 1), (dest - x) & (SIDE - 1)
            first, second = jnp.where(core == 0, dy, dx), jnp.where(core == 0, dx, dy)
            owner = first * SIDE + second
            rank = count[owner]
            count[owner] = rank + 1
            rows[owner, rank] = index_ref[group + 1, t]

            def send(d, t=t, second=second, rank=rank):
                for c in range(CHUNKS):
                    copy_out(t, d, second, rank, c).start()

            one_of(first, 0, SIDE, send)
        return carry

    lax.fori_loop(0, targets // UNROLL, several, 0)
    lane = lax.broadcasted_iota(jnp.int32, (META, width), 1)
    for o in range(OWNERS):
        values = jnp.full((META, width), -1, jnp.int32)
        for r in range(CAP):
            values = jnp.where(lane == r, rows[o, r], values)
        meta[o] = values.astype(F32).astype(BF16)
    tails = [
        pltpu.make_async_copy(
            meta.at[pl.ds(d * SIDE, SIDE)],
            outs[c * SIDE + d].at[:, pl.ds(CAP * BS, META), :],
            meta_sems.at[c, d],
        )
        for c in range(CHUNKS)
        for d in range(SIDE)
    ]
    for tail in tails:
        tail.start()

    def finish(t, carry):
        for c in range(CHUNKS):
            copy_out(t, 0, 0, 0, c).wait()
        return carry

    lax.fori_loop(0, targets, finish, 0)
    for tail in tails:
        tail.wait()


def partials(a_blocks, omega, route_dest, row_target, col_target, place):
    targets = col_target.shape[0]
    width = omega.shape[1]
    slab = omega.reshape(-1, BS, width)
    indices = jnp.concatenate([col_target.T, route_dest.T, row_target[None, :]])
    out = jax.ShapeDtypeStruct((SIDE, SLOT_ROWS, width // CHUNKS), BF16)
    outs = pl.pallas_call(
        partial_kernel,
        in_specs=[SCALARS] * 2 + [IN_HBM] * 2,
        out_specs=[pl.BlockSpec(memory_space=pl.ANY)] * (CHUNKS * SIDE),
        out_shape=[out] * (CHUNKS * SIDE),
        scratch_shapes=[
            pltpu.VMEM(a_blocks.shape, BF16),
            pltpu.VMEM(slab.shape, BF16),
            pltpu.VMEM((targets, BS, width), BF16),
            pltpu.VMEM((OWNERS, META, width // CHUNKS), BF16),
            pltpu.SMEM((OWNERS, CAP), jnp.int32),
            pltpu.SMEM((OWNERS,), jnp.int32),
            pltpu.SemaphoreType.DMA((targets // UNROLL,)),
            pltpu.SemaphoreType.DMA,
            pltpu.SemaphoreType.DMA((CHUNKS, targets)),
            pltpu.SemaphoreType.DMA((CHUNKS, SIDE)),
        ],
        compiler_params=pltpu.CompilerParams(vmem_limit_bytes=48 * MIB),
        name="partials",
    )(indices, place, a_blocks, slab)
    return [outs[c * SIDE : (c + 1) * SIDE] for c in range(CHUNKS)]


def slot_sum_kernel(place_ref, *refs):
    got, (send_ref, acc, ints, rows, sem) = refs[: 2 * SIDE - 1], refs[2 * SIDE - 1 :]
    z, core = place_ref[0], place_ref[1]
    pieces = [(ref, 0) for ref in got[:SIDE]] + [(ref, i) for ref in got[SIDE:] for i in range(SIDE)]
    for s, (ref, i) in enumerate(pieces):
        tile = ref[i, CAP * BS : SLOT_ROWS, 0:BS].astype(F32)
        row = tile[0:1, :].astype(jnp.int32)
        side = (row // RB_DEV) & 1
        chip = (row // (2 * RB_DEV) - z) & (SIDE - 1)
        place = jnp.where(side == core, 0, HALF) + chip * RB_DEV + (row & (RB_DEV - 1))
        ints[s : s + 1, :] = jnp.where(row < 0, row, place)
    copy = pltpu.make_async_copy(ints, rows, sem)
    copy.start()

    def clear(b, carry):
        acc[b] = jnp.zeros(acc.shape[1:], F32)
        return carry

    lax.fori_loop(0, 2 * HALF, clear, 0, unroll=2)
    copy.wait()
    for s, (ref, i) in enumerate(pieces):
        for r in range(CAP):
            place = rows[s, r]

            @pl.when(place >= 0)
            def _():
                acc[place] = acc[place] + ref[i, r * BS : (r + 1) * BS, :].astype(F32)

    def write(k, carry):
        send_ref[k] = acc[HALF + k].astype(BF16)
        return carry

    lax.fori_loop(0, HALF, write, 0, unroll=2)


def slot_sums(place, got):
    width = got[0].shape[2]
    return pl.pallas_call(
        slot_sum_kernel,
        in_specs=[SCALARS] + [WHOLE] * len(got),
        out_specs=[WHOLE] * 2,
        out_shape=[
            jax.ShapeDtypeStruct((HALF, BS, width), BF16),
            jax.ShapeDtypeStruct((2 * HALF, BS, width), F32),
        ],
        scratch_shapes=[
            pltpu.VMEM((OWNERS, BS), jnp.int32),
            pltpu.SMEM((OWNERS, BS), jnp.int32),
            pltpu.SemaphoreType.DMA,
        ],
        compiler_params=pltpu.CompilerParams(vmem_limit_bytes=22 * MIB),
        name="slot_sums",
    )(place, *got)


def gram_kernel(place_ref, *refs):
    parts, (sketch_ref, send_ref, keep_ref, gram) = refs[: 5 * CHUNKS], refs[5 * CHUNKS :]
    core = place_ref[1]
    width = parts[0].shape[1]
    for c in range(CHUNKS):
        own, from_core, one, two, three = (ref[...].astype(F32) for ref in parts[5 * c : 5 * c + 5])
        sketch_ref[:, c * width : (c + 1) * width] = (own + from_core) + (one + three) + two
    sketch = sketch_ref[...]
    gram[...] = lax.dot_general(
        sketch, sketch, (((0,), (0,)), ((), ())), precision=HIGHEST, preferred_element_type=F32
    )
    for side, (upper_ref, lower_ref) in enumerate(((keep_ref, send_ref), (send_ref, keep_ref))):

        @pl.when(core == side)
        def _():
            upper_ref[0:BS, :] = gram[0:BS, 0:BS]
            upper_ref[BS:, :] = gram[0 : BS // 2, BS:]
            lower_ref[0:BS, :] = gram[BS:, BS:]
            lower_ref[BS:, :] = gram[BS // 2 : BS, BS:]


def gram_halves(place, parts):
    rows = RB_DEV * BS
    width = CHUNKS * parts[0].shape[1]
    return pl.pallas_call(
        gram_kernel,
        in_specs=[SCALARS] + [WHOLE] * (5 * CHUNKS),
        out_specs=[WHOLE] * 3,
        out_shape=[
            jax.ShapeDtypeStruct((rows, width), F32),
            jax.ShapeDtypeStruct((BS + BS // 2, BS), F32),
            jax.ShapeDtypeStruct((BS + BS // 2, BS), F32),
        ],
        scratch_shapes=[pltpu.VMEM((width, width), F32)],
        compiler_params=pltpu.CompilerParams(vmem_limit_bytes=20 * MIB),
        name="sum_gram",
    )(place, *parts)


def small_factor(block):
    n = len(block)
    low = [list(row) for row in block]
    inv = [None] * n
    for k in range(n):
        inv[k] = lax.rsqrt(low[k][k])
        for i in range(k + 1, n):
            low[i][k] = low[i][k] * inv[k]
        for j in range(k + 1, n):
            for i in range(j, n):
                low[i][j] = low[i][j] - low[i][k] * low[j][k]
    out = [[None] * n for _ in range(n)]
    for j in range(n):
        out[j][j] = inv[j]
        for i in range(j + 1, n):
            s = low[i][j] * out[j][j]
            for m in range(j + 1, i):
                s = s + low[i][m] * out[m][j]
            out[i][j] = -(s * inv[i])
    return out


def wide(value):
    return jnp.broadcast_to(value, (8, BS))


def factor_panel(panel, lane, meanwhile):
    sub = lax.broadcasted_iota(jnp.int32, (8, BS), 0)
    for g in range(len(panel)):
        at = lane + 8 * g
        cols = [wide(panel[g][0][:, at + c : at + c + 1]) for c in range(8)]
        inverse = small_factor([[wide(cols[c][r : r + 1, :]) for c in range(r + 1)] for r in range(8)])
        spread = []
        for k in range(8):
            value = inverse[7][k]
            for r in range(6, k - 1, -1):
                value = jnp.where(sub == r, inverse[r][k], value)
            spread.append(jnp.where(sub >= k, value, 0.0))
        done = []
        for tile in panel[g]:
            total = spread[0] * wide(tile[0:1, :])
            for k in range(1, 8):
                total = total + spread[k] * wide(tile[k : k + 1, :])
            done.append(total)
        panel[g] = done
        done_rows = [[wide(tile[k : k + 1, :]) for k in range(8)] for tile in done]
        if g == 0:
            meanwhile()
        for h in range(g + 1, len(panel)):
            cols = [wide(panel[h][0][:, at + c : at + c + 1]) for c in range(8)]
            for k in range(8):
                ratio = cols[0] * inverse[k][0]
                for m in range(1, k + 1):
                    ratio = ratio + cols[m] * inverse[k][m]
                for t in range(len(done)):
                    panel[h][t] = panel[h][t] - ratio * done_rows[t][k]


def factor_kernel(scale, place_ref, mine_ref, other_ref, sketch_ref, basis_ref, factor_ref, work):
    core = place_ref[1]
    n = factor_ref.shape[1]
    work[BS:, 0:BS] = jnp.zeros((BS, BS), F32)
    for side, (upper_ref, lower_ref) in enumerate(((mine_ref, other_ref), (other_ref, mine_ref))):

        @pl.when(core == side)
        def _():
            work[0:BS, 0:BS] = upper_ref[0:BS, :]
            work[0 : BS // 2, BS:n] = upper_ref[BS:, :]
            work[BS:n, BS:n] = lower_ref[0:BS, :]
            work[BS // 2 : BS, BS:n] = lower_ref[BS:, :]

    down = lax.broadcasted_iota(jnp.int32, (n, n), 0)
    across = lax.broadcasted_iota(jnp.int32, (n, n), 1)
    work[:, n : 2 * n] = (down == across).astype(F32)

    def update(j, low, high):
        if low < high:
            first, last = (j // BS) * BS, n + (j // BS) * BS + BS
            work[low:high, first:last] -= lax.dot_general(
                work[j : j + PANEL, low:high],
                work[j : j + PANEL, first:last],
                (((0,), (0,)), ((), ())),
                precision=HIGHEST,
                preferred_element_type=F32,
            )

    for j in range(0, n, PANEL):
        first, last = (j // BS) * BS, n + (j // BS) * BS + BS
        tiles = range(first, last, BS)
        panel = [[work[i : i + 8, t : t + BS] for t in tiles] for i in range(j, j + PANEL, 8)]
        factor_panel(panel, j - first, functools.partial(update, j - PANEL, j + PANEL, n if j else 0))
        for g, group in enumerate(panel):
            for t, tile in zip(tiles, group):
                work[j + 8 * g : j + 8 * g + 8, t : t + BS] = tile
        update(j, j + PANEL, min(j + 2 * PANEL, n))
    factor_ref[...] = jnp.where(down <= across, work[:, 0:n], 0.0) * (1.0 / scale)
    inverse = work[:, n : 2 * n] * scale
    basis_ref[...] = lax.dot_general(
        sketch_ref[...], inverse, (((1,), (1,)), ((), ())), precision=HIGHEST, preferred_element_type=F32
    )


def factors(scale, place, mine, other, sketch):
    rows, width = sketch.shape
    return pl.pallas_call(
        functools.partial(factor_kernel, scale),
        in_specs=[SCALARS] + [WHOLE] * 3,
        out_specs=[WHOLE] * 2,
        out_shape=[
            jax.ShapeDtypeStruct((rows, width), F32),
            jax.ShapeDtypeStruct((width, width), F32),
        ],
        scratch_shapes=[pltpu.VMEM((width, 2 * width), F32)],
        compiler_params=pltpu.CompilerParams(vmem_limit_bytes=16 * MIB),
        name="factor_basis",
    )(place, mine, other, sketch)


def other_core(value):
    return lax.ppermute(value, "col", [(i, i ^ 1) for i in range(2 * SIDE)])


def moved(value, target):
    pairs = []
    for y in range(SIDE):
        for x in range(SIDE):
            for z in range(SIDE):
                for core in range(2):
                    to_y, to_x, to_z = target(core, (y, x, z))
                    source = ((y * SIDE + x) * SIDE + z) * 2 + core
                    pairs.append((source, ((to_y * SIDE + to_x) * SIDE + to_z) * 2 + core))
    return lax.ppermute(value, ("row", "col"), pairs)


def along(value, axes, step):
    def target(core, chip):
        return tuple(step(at) if axis == axes[core] else at for axis, at in enumerate(chip))

    return moved(value, target)


def ahead(value, axes, d):
    return along(value, axes, lambda at: (at + d) % SIDE)


def summed(value):
    for axes in ((2, 0), (0, 1), (1, 2)):
        one, three, two = (ahead(value, axes, d) for d in (1, 3, 2))
        value = (value + two) + (one + three)
    return value


def body(scale, a_blocks, omega, route_dest, row_target, col_target):
    row, col = lax.axis_index("row"), lax.axis_index("col")
    place = jnp.stack([col // 2, col % 2, row // SIDE, row % SIDE]).astype(jnp.int32)
    sends = partials(a_blocks, omega, route_dest, row_target, col_target, place)
    parts = []
    for c, send in enumerate(sends):
        near = [send[0]] + [ahead(send[d], (0, 1), d) for d in (1, 3, 2)]
        across = [jnp.stack([part[d] for part in near]) for d in (1, 3, 2)]
        far = [ahead(value, (1, 0), d) for d, value in zip((1, 3, 2), across)]
        kept, leaving = core_sums(place, near + far)
        parts = parts + kept + sent_along_z(leaving)
    sketch, gram_send, gram_keep = gram_halves(place, parts)
    gram = summed(gram_keep + other_core(gram_send))
    return tuple(factors(scale, place, gram, other_core(gram), sketch))


def core_sums(place, got):
    to_core, own = slot_sums(place, got)
    width = own.shape[-1]
    own, from_core = own.reshape(2 * SIDE, -1, width), other_core(to_core).reshape(SIDE, -1, width)
    leaving = [(own[d] + from_core[d].astype(F32)).astype(BF16) for d in (1, 3, 2)]
    return [own[0], from_core[0]], leaving


def sent_along_z(leaving):
    return [ahead(value, (2, 2), d) for d, value in zip((1, 3, 2), leaving)]


def solution(mesh):
    rows_total = mesh.shape["row"] * mesh.shape["col"] * RB_DEV * BS
    return jax.shard_map(
        functools.partial(body, float(rows_total) ** 0.5),
        mesh=mesh,
        in_specs=(
            P(("row", "col"), None, None, None),
            P("col", None),
            P(("row", "col"), None),
            P(("row", "col")),
            P(("row", "col"), None),
        ),
        out_specs=(P(("row", "col"), None), P()),
        check_vma=False,
    )
```

```python
import functools

import jax
import jax.numpy as jnp
from jax import lax
from jax.experimental import pallas as pl
from jax.experimental.pallas import tpu as pltpu
from jax.sharding import PartitionSpec as P

RB_DEV = 8
CAP = 4
BS = 128
META = 16
SLOT_ROWS = CAP * BS + META
CHUNKS = 2
CARRIER = CHUNKS - 1
PANEL = 32
UNROLL = 4
AHEAD = 3
SIDE = 4
OWNERS = SIDE * SIDE
HALF = SIDE * RB_DEV
F32 = jnp.float32
BF16 = jnp.bfloat16
HIGHEST = lax.Precision.HIGHEST
MIB = 1024 * 1024
WHOLE = pl.BlockSpec(memory_space=pltpu.VMEM)
SCALARS = pl.BlockSpec(memory_space=pltpu.SMEM)
IN_HBM = pl.BlockSpec(memory_space=pltpu.HBM)


def one_of(index, low, high, act):
    if high - low == 1:
        act(low)
        return
    middle = (low + high) // 2
    lax.cond(
        index < middle,
        lambda: one_of(index, low, middle, act),
        lambda: one_of(index, middle, high, act),
    )


def partial_kernel(index_ref, place_ref, a_ref, omega_ref, *refs):
    outs, scratch = refs[: CHUNKS * SIDE], refs[CHUNKS * SIDE :]
    blocks, slab, stage, meta, rows, count, a_sems, slab_sem, out_sems, meta_sems = scratch
    targets, group = blocks.shape[:2]
    width = slab.shape[-1] // CHUNKS
    core, y, x = place_ref[1], place_ref[2], place_ref[3]
    slab_copy = pltpu.make_async_copy(omega_ref, slab, slab_sem)
    slab_copy.start()

    def load(step):
        some = pl.ds(step * UNROLL, UNROLL)
        return pltpu.make_async_copy(a_ref.at[some], blocks.at[some], a_sems.at[step])

    for step in range(AHEAD):
        load(step).start()

    def clear(o, carry):
        count[o] = 0
        for r in range(CAP):
            rows[o, r] = -1
        return carry

    lax.fori_loop(0, OWNERS, clear, 0)
    slab_copy.wait()

    def copy_out(t, first, second, rank, c):
        return pltpu.make_async_copy(
            stage.at[t, :, pl.ds(c * width, width)],
            outs[c * SIDE + first].at[second, pl.ds(pl.multiple_of(rank * BS, BS), BS), :],
            out_sems.at[c, t],
        )

    def several(step, carry):
        @pl.when(step + AHEAD < targets // UNROLL)
        def _():
            load(step + AHEAD).start()

        load(step).wait()
        for i in range(UNROLL):
            t = step * UNROLL + i
            left = jnp.concatenate([blocks[t, g] for g in range(group)], axis=1)
            right = jnp.concatenate([slab[index_ref[g, t]] for g in range(group)], axis=0)
            stage[t] = jnp.dot(left, right, preferred_element_type=F32).astype(BF16)
        for i in range(UNROLL):
            t = step * UNROLL + i
            dest = index_ref[group, t]
            dy, dx = (dest // SIDE - y) & (SIDE - 1), (dest - x) & (SIDE - 1)
            first, second = jnp.where(core == 0, dy, dx), jnp.where(core == 0, dx, dy)
            owner = first * SIDE + second
            rank = count[owner]
            count[owner] = rank + 1
            rows[owner, rank] = index_ref[group + 1, t]

            def send(d, t=t, second=second, rank=rank):
                for c in range(CHUNKS):
                    copy_out(t, d, second, rank, c).start()

            one_of(first, 0, SIDE, send)
        return carry

    lax.fori_loop(0, targets // UNROLL, several, 0)
    lane = lax.broadcasted_iota(jnp.int32, (META, width), 1)
    for o in range(OWNERS):
        values = jnp.full((META, width), -1, jnp.int32)
        for r in range(CAP):
            values = jnp.where(lane == r, rows[o, r], values)
        meta[o] = values.astype(F32).astype(BF16)
    tails = [
        pltpu.make_async_copy(
            meta.at[pl.ds(d * SIDE, SIDE)],
            outs[CARRIER * SIDE + d].at[:, pl.ds(CAP * BS, META), :],
            meta_sems.at[d],
        )
        for d in range(SIDE)
    ]
    for tail in tails:
        tail.start()

    def finish(t, carry):
        for c in range(CHUNKS):
            copy_out(t, 0, 0, 0, c).wait()
        return carry

    lax.fori_loop(0, targets, finish, 0)
    for tail in tails:
        tail.wait()


def partials(a_blocks, omega, route_dest, row_target, col_target, place):
    targets = col_target.shape[0]
    width = omega.shape[1]
    slab = omega.reshape(-1, BS, width)
    indices = jnp.concatenate([col_target.T, route_dest.T, row_target[None, :]])
    out_shape = [
        jax.ShapeDtypeStruct((SIDE, SLOT_ROWS if c == CARRIER else CAP * BS, width // CHUNKS), BF16)
        for c in range(CHUNKS)
        for _ in range(SIDE)
    ]
    outs = pl.pallas_call(
        partial_kernel,
        in_specs=[SCALARS] * 2 + [IN_HBM] * 2,
        out_specs=[pl.BlockSpec(memory_space=pl.ANY)] * (CHUNKS * SIDE),
        out_shape=out_shape,
        scratch_shapes=[
            pltpu.VMEM(a_blocks.shape, BF16),
            pltpu.VMEM(slab.shape, BF16),
            pltpu.VMEM((targets, BS, width), BF16),
            pltpu.VMEM((OWNERS, META, width // CHUNKS), BF16),
            pltpu.SMEM((OWNERS, CAP), jnp.int32),
            pltpu.SMEM((OWNERS,), jnp.int32),
            pltpu.SemaphoreType.DMA((targets // UNROLL,)),
            pltpu.SemaphoreType.DMA,
            pltpu.SemaphoreType.DMA((CHUNKS, targets)),
            pltpu.SemaphoreType.DMA((SIDE,)),
        ],
        compiler_params=pltpu.CompilerParams(vmem_limit_bytes=48 * MIB),
        name="partials",
    )(indices, place, a_blocks, slab)
    return [outs[c * SIDE : (c + 1) * SIDE] for c in range(CHUNKS)]


def carrier_sum_kernel(place_ref, *refs):
    got, (send_ref, acc, ints, rows, sem) = refs[: 2 * SIDE - 1], refs[2 * SIDE - 1 :]
    z, core = place_ref[0], place_ref[1]
    for s, (ref, i) in enumerate(slots_of(got)):
        tile = ref[i, CAP * BS : SLOT_ROWS, 0:BS].astype(F32)
        row = tile[0:1, :].astype(jnp.int32)
        side = (row // RB_DEV) & 1
        chip = (row // (2 * RB_DEV) - z) & (SIDE - 1)
        place = jnp.where(side == core, 0, HALF) + chip * RB_DEV + (row & (RB_DEV - 1))
        ints[s : s + 1, :] = jnp.where(row < 0, row, place)
    copy = pltpu.make_async_copy(ints, rows, sem)
    copy.start()
    copy.wait()
    add_slots(rows, got, send_ref, acc)


def slot_sum_kernel(rows, *refs):
    got, (send_ref, acc) = refs[: 2 * SIDE - 1], refs[2 * SIDE - 1 :]
    add_slots(rows, got, send_ref, acc)


def slots_of(got):
    return [(ref, 0) for ref in got[:SIDE]] + [(ref, i) for ref in got[SIDE:] for i in range(SIDE)]


def add_slots(rows, got, send_ref, acc):
    def clear(b, carry):
        acc[b] = jnp.zeros(acc.shape[1:], F32)
        return carry

    lax.fori_loop(0, 2 * HALF, clear, 0, unroll=2)
    for s, (ref, i) in enumerate(slots_of(got)):
        for r in range(CAP):
            place = rows[s, r]

            @pl.when(place >= 0)
            def _():
                acc[place] = acc[place] + ref[i, r * BS : (r + 1) * BS, :].astype(F32)

    def write(k, carry):
        send_ref[k] = acc[HALF + k].astype(BF16)
        return carry

    lax.fori_loop(0, HALF, write, 0, unroll=2)


def slot_sums(place, got, rows):
    width = got[0].shape[2]
    carrier = rows is None
    out_shape = [
        jax.ShapeDtypeStruct((HALF, BS, width), BF16),
        jax.ShapeDtypeStruct((2 * HALF, BS, width), F32),
        jax.ShapeDtypeStruct((OWNERS, BS), jnp.int32),
    ]
    outs = pl.pallas_call(
        carrier_sum_kernel if carrier else slot_sum_kernel,
        in_specs=[SCALARS] + [WHOLE] * len(got),
        out_specs=[WHOLE] * (3 if carrier else 2),
        out_shape=out_shape if carrier else out_shape[:2],
        scratch_shapes=[pltpu.SMEM((OWNERS, BS), jnp.int32), pltpu.SemaphoreType.DMA] if carrier else [],
        compiler_params=pltpu.CompilerParams(vmem_limit_bytes=22 * MIB),
        name="carrier_sums" if carrier else "slot_sums",
    )(place if carrier else rows, *got)
    return outs if carrier else [*outs, rows]


def gram_kernel(place_ref, *refs):
    parts, (sketch_ref, send_ref, keep_ref, gram) = refs[: 5 * CHUNKS], refs[5 * CHUNKS :]
    core = place_ref[1]
    width = parts[0].shape[1]
    for c in range(CHUNKS):
        own, from_core, one, two, three = (ref[...].astype(F32) for ref in parts[5 * c : 5 * c + 5])
        sketch_ref[:, c * width : (c + 1) * width] = (own + from_core) + (one + three) + two
    sketch = sketch_ref[...]
    gram[...] = lax.dot_general(
        sketch, sketch, (((0,), (0,)), ((), ())), precision=HIGHEST, preferred_element_type=F32
    )
    for side, (upper_ref, lower_ref) in enumerate(((keep_ref, send_ref), (send_ref, keep_ref))):

        @pl.when(core == side)
        def _():
            upper_ref[0:BS, :] = gram[0:BS, 0:BS]
            upper_ref[BS:, :] = gram[0 : BS // 2, BS:]
            lower_ref[0:BS, :] = gram[BS:, BS:]
            lower_ref[BS:, :] = gram[BS // 2 : BS, BS:]


def gram_halves(place, parts):
    rows = RB_DEV * BS
    width = CHUNKS * parts[0].shape[1]
    return pl.pallas_call(
        gram_kernel,
        in_specs=[SCALARS] + [WHOLE] * (5 * CHUNKS),
        out_specs=[WHOLE] * 3,
        out_shape=[
            jax.ShapeDtypeStruct((rows, width), F32),
            jax.ShapeDtypeStruct((BS + BS // 2, BS), F32),
            jax.ShapeDtypeStruct((BS + BS // 2, BS), F32),
        ],
        scratch_shapes=[pltpu.VMEM((width, width), F32)],
        compiler_params=pltpu.CompilerParams(vmem_limit_bytes=20 * MIB),
        name="sum_gram",
    )(place, *parts)


def small_factor(block):
    n = len(block)
    low = [list(row) for row in block]
    inv = [None] * n
    for k in range(n):
        inv[k] = lax.rsqrt(low[k][k])
        for i in range(k + 1, n):
            low[i][k] = low[i][k] * inv[k]
        for j in range(k + 1, n):
            for i in range(j, n):
                low[i][j] = low[i][j] - low[i][k] * low[j][k]
    out = [[None] * n for _ in range(n)]
    for j in range(n):
        out[j][j] = inv[j]
        for i in range(j + 1, n):
            s = low[i][j] * out[j][j]
            for m in range(j + 1, i):
                s = s + low[i][m] * out[m][j]
            out[i][j] = -(s * inv[i])
    return out


def wide(value):
    return jnp.broadcast_to(value, (8, BS))


def factor_panel(panel, lane, meanwhile):
    sub = lax.broadcasted_iota(jnp.int32, (8, BS), 0)
    for g in range(len(panel)):
        at = lane + 8 * g
        cols = [wide(panel[g][0][:, at + c : at + c + 1]) for c in range(8)]
        inverse = small_factor([[wide(cols[c][r : r + 1, :]) for c in range(r + 1)] for r in range(8)])
        spread = []
        for k in range(8):
            value = inverse[7][k]
            for r in range(6, k - 1, -1):
                value = jnp.where(sub == r, inverse[r][k], value)
            spread.append(jnp.where(sub >= k, value, 0.0))
        done = []
        for tile in panel[g]:
            total = spread[0] * wide(tile[0:1, :])
            for k in range(1, 8):
                total = total + spread[k] * wide(tile[k : k + 1, :])
            done.append(total)
        panel[g] = done
        done_rows = [[wide(tile[k : k + 1, :]) for k in range(8)] for tile in done]
        if g == 0:
            meanwhile()
        for h in range(g + 1, len(panel)):
            cols = [wide(panel[h][0][:, at + c : at + c + 1]) for c in range(8)]
            for k in range(8):
                ratio = cols[0] * inverse[k][0]
                for m in range(1, k + 1):
                    ratio = ratio + cols[m] * inverse[k][m]
                for t in range(len(done)):
                    panel[h][t] = panel[h][t] - ratio * done_rows[t][k]


def factor_kernel(scale, place_ref, mine_ref, other_ref, sketch_ref, basis_ref, factor_ref, work):
    core = place_ref[1]
    n = factor_ref.shape[1]
    work[BS:, 0:BS] = jnp.zeros((BS, BS), F32)
    for side, (upper_ref, lower_ref) in enumerate(((mine_ref, other_ref), (other_ref, mine_ref))):

        @pl.when(core == side)
        def _():
            work[0:BS, 0:BS] = upper_ref[0:BS, :]
            work[0 : BS // 2, BS:n] = upper_ref[BS:, :]
            work[BS:n, BS:n] = lower_ref[0:BS, :]
            work[BS // 2 : BS, BS:n] = lower_ref[BS:, :]

    down = lax.broadcasted_iota(jnp.int32, (n, n), 0)
    across = lax.broadcasted_iota(jnp.int32, (n, n), 1)
    work[:, n : 2 * n] = (down == across).astype(F32)

    def update(j, low, high):
        if low < high:
            first, last = (j // BS) * BS, n + (j // BS) * BS + BS
            work[low:high, first:last] -= lax.dot_general(
                work[j : j + PANEL, low:high],
                work[j : j + PANEL, first:last],
                (((0,), (0,)), ((), ())),
                precision=HIGHEST,
                preferred_element_type=F32,
            )

    for j in range(0, n, PANEL):
        first, last = (j // BS) * BS, n + (j // BS) * BS + BS
        tiles = range(first, last, BS)
        panel = [[work[i : i + 8, t : t + BS] for t in tiles] for i in range(j, j + PANEL, 8)]
        factor_panel(panel, j - first, functools.partial(update, j - PANEL, j + PANEL, n if j else 0))
        for g, group in enumerate(panel):
            for t, tile in zip(tiles, group):
                work[j + 8 * g : j + 8 * g + 8, t : t + BS] = tile
        update(j, j + PANEL, min(j + 2 * PANEL, n))
    factor_ref[...] = jnp.where(down <= across, work[:, 0:n], 0.0) * (1.0 / scale)
    inverse = work[:, n : 2 * n] * scale
    basis_ref[...] = lax.dot_general(
        sketch_ref[...], inverse, (((1,), (1,)), ((), ())), precision=HIGHEST, preferred_element_type=F32
    )


def factors(scale, place, mine, other, sketch):
    rows, width = sketch.shape
    return pl.pallas_call(
        functools.partial(factor_kernel, scale),
        in_specs=[SCALARS] + [WHOLE] * 3,
        out_specs=[WHOLE] * 2,
        out_shape=[
            jax.ShapeDtypeStruct((rows, width), F32),
            jax.ShapeDtypeStruct((width, width), F32),
        ],
        scratch_shapes=[pltpu.VMEM((width, 2 * width), F32)],
        compiler_params=pltpu.CompilerParams(vmem_limit_bytes=16 * MIB),
        name="factor_basis",
    )(place, mine, other, sketch)


def other_core(value):
    return lax.ppermute(value, "col", [(i, i ^ 1) for i in range(2 * SIDE)])


def moved(value, target):
    pairs = []
    for y in range(SIDE):
        for x in range(SIDE):
            for z in range(SIDE):
                for core in range(2):
                    to_y, to_x, to_z = target(core, (y, x, z))
                    source = ((y * SIDE + x) * SIDE + z) * 2 + core
                    pairs.append((source, ((to_y * SIDE + to_x) * SIDE + to_z) * 2 + core))
    return lax.ppermute(value, ("row", "col"), pairs)


def along(value, axes, step):
    def target(core, chip):
        return tuple(step(at) if axis == axes[core] else at for axis, at in enumerate(chip))

    return moved(value, target)


def ahead(value, axes, d):
    return along(value, axes, lambda at: (at + d) % SIDE)


def summed(value):
    for axes in ((2, 0), (0, 1), (1, 2)):
        one, three, two = (ahead(value, axes, d) for d in (1, 3, 2))
        value = (value + two) + (one + three)
    return value


def body(scale, a_blocks, omega, route_dest, row_target, col_target):
    row, col = lax.axis_index("row"), lax.axis_index("col")
    place = jnp.stack([col // 2, col % 2, row // SIDE, row % SIDE]).astype(jnp.int32)
    sends = partials(a_blocks, omega, route_dest, row_target, col_target, place)
    parts = []
    rows = None
    for send in sends[::-1]:
        near = [send[0]] + [ahead(send[d], (0, 1), d) for d in (1, 3, 2)]
        across = [jnp.stack([part[d] for part in near]) for d in (1, 3, 2)]
        far = [ahead(value, (1, 0), d) for d, value in zip((1, 3, 2), across)]
        kept, leaving, rows = core_sums(place, near + far, rows)
        parts = kept + sent_along_z(leaving) + parts
    sketch, gram_send, gram_keep = gram_halves(place, parts)
    gram = summed(gram_keep + other_core(gram_send))
    return tuple(factors(scale, place, gram, other_core(gram), sketch))


def core_sums(place, got, rows):
    to_core, own, rows = slot_sums(place, got, rows)
    width = own.shape[-1]
    own, from_core = own.reshape(2 * SIDE, -1, width), other_core(to_core).reshape(SIDE, -1, width)
    leaving = [(own[d] + from_core[d].astype(F32)).astype(BF16) for d in (1, 3, 2)]
    return [own[0], from_core[0]], leaving, rows


def sent_along_z(leaving):
    return [ahead(value, (2, 2), d) for d, value in zip((1, 3, 2), leaving)]


def solution(mesh):
    rows_total = mesh.shape["row"] * mesh.shape["col"] * RB_DEV * BS
    return jax.shard_map(
        functools.partial(body, float(rows_total) ** 0.5),
        mesh=mesh,
        in_specs=(
            P(("row", "col"), None, None, None),
            P("col", None),
            P(("row", "col"), None),
            P(("row", "col")),
            P(("row", "col"), None),
        ),
        out_specs=(P(("row", "col"), None), P()),
        check_vma=False,
    )
```
